32 devices in a mesh: dp: 8 (over z, x), ctx: 4 (over y, core).
Axes of the slice: x: 2, y: 2, z: 4, core: 2. Of those that a mesh axis runs over, the one named last changes fastest.
Arguments:
- prompt_q: bfloat16 [8, 512, 4096], P('dp', 'ctx'), may hold values from -260 to 260
- prompt_k: bfloat16 [8, 512, 512], P('dp', 'ctx'), may hold values from -8 to 8
- prompt_v: bfloat16 [8, 512, 512], P('dp', 'ctx'), may hold values from -12 to 12
- prompt_len: int32 [8], P('dp'), may hold values from 256 to 512
- resp_q: bfloat16 [8, 128, 4096], P('dp', 'ctx'), may hold values from -260 to 260
- resp_k: bfloat16 [8, 128, 512], P('dp', 'ctx'), may hold values from -6 to 6
- resp_v: bfloat16 [8, 128, 512], P('dp', 'ctx'), may hold values from -12 to 12
- resp_len: int32 [8, 8], P('dp', 'ctx'), may hold values from 1 to 16
- resp_resid: bfloat16 [8, 128, 4096], P('dp', 'ctx'), may hold values from -4 to 4
- norm_gain: float32 [4096], replicated, may hold values from 0.5 to 1.5
- gate_weight: bfloat16 [4096, 14336], P('dp', 'ctx'), may hold values from -0.09375 to 0.09375
- up_weight: bfloat16 [4096, 14336], P('dp', 'ctx'), may hold values from -0.09375 to 0.09375
Outputs:
- prompt_attn: bfloat16 [8, 512, 4096], P('dp', 'ctx')
- resp_hidden: bfloat16 [8, 128, 14336], P('dp', None, 'ctx')
The draws below stay inside these ranges and needn't reach their ends.
All inputs are finite; a program needn't handle non-finite values.
Results may differ from the reference program's by a relative error of at most 0.012.
Values may be sent and summed in bfloat16 or wider, within the bound.
A program may use at most 128 MiB of HBM per device.

```python
import jax
import jax.numpy as jnp
from jax import lax

QUERY_HEADS = 32
KEY_VALUE_HEADS = 4
HEAD_SIZE = 128
D = 4096
KVW = 512
FF = 14336
RLEN = 16
PROMPT_POSITIONS = 512
RESP = 128
PROMPT_GROUPS = 8
N_CTX = 4


def marked_keys(key):
    base_offset = jax.random.fold_in(key, 11)
    key_matrix = jnp.clip(jax.random.normal(base_offset, (PROMPT_GROUPS, PROMPT_POSITIONS, KEY_VALUE_HEADS * HEAD_SIZE), jnp.float32), -6.0, 6.0)
    return key_matrix


def draw_prompt_k(key, part):
    key_matrix = marked_keys(key)
    return key_matrix.astype(jnp.bfloat16)


def draw_prompt_q(key, part):
    base_offset = jax.random.fold_in(key, 13)
    queries = 1.5 * jnp.clip(jax.random.normal(base_offset, (PROMPT_GROUPS, PROMPT_POSITIONS, QUERY_HEADS * HEAD_SIZE), jnp.float32), -6.0, 6.0)
    return queries.astype(jnp.bfloat16)


def draw_resp_q(key, part):
    base_offset = jax.random.fold_in(key, 14)
    queries = 1.5 * jnp.clip(jax.random.normal(base_offset, (PROMPT_GROUPS, RESP, QUERY_HEADS * HEAD_SIZE), jnp.float32), -6.0, 6.0)
    return queries.astype(jnp.bfloat16)


def touch_ends(values, rng, low, largest):
    place = [jax.random.randint(jax.random.fold_in(rng, axis), (), 0, length) for axis, length in enumerate(values.shape)]
    longest = values.shape.index(max(values.shape))
    neighbour = place[:longest] + [(place[longest] + 1) % values.shape[longest]] + place[longest + 1:]
    return values.at[tuple(place)].set(low).at[tuple(neighbour)].set(largest)


def shard_levels(rng, extent, cuts, least, top_value):
    def one(position, parts):
        draws = jax.random.uniform(jax.random.fold_in(jax.random.fold_in(rng, 6), position), (parts,), jnp.float32, least / len(cuts), top_value / len(cuts))
        return jnp.repeat(jnp.exp(draws), extent[position] // parts).reshape((-1,) + (1,) * (len(extent) - position - 1))

    level = one(*cuts[0])
    for cut in cuts[1:]:
        level = level * one(*cut)
    return level


def normal_values(key, extent, width, most, split=(), kind=jnp.bfloat16):
    values = width * jax.random.normal(key, extent, jnp.float32)
    if split:
        values = values * shard_levels(key, extent, split, -0.22, 0.18)
    return jnp.clip(values, -most, most).astype(kind)


def setup_inputs(seed: int = 0) -> dict:
    key_of = jax.random.split(jax.random.key(seed), 13)
    prompt_q = draw_prompt_q(jax.random.fold_in(key_of[12], 71), 0)
    prompt_k = draw_prompt_k(jax.random.fold_in(key_of[12], 71), 0)
    prompt_v = normal_values(key_of[2], (PROMPT_GROUPS, PROMPT_POSITIONS, KVW), 2.0, 12.0, ((0, 8), (1, 4)))
    prompt_len = touch_ends(jax.random.randint(key_of[3], (PROMPT_GROUPS,), PROMPT_POSITIONS // 2, PROMPT_POSITIONS + 1), jax.random.fold_in(key_of[3], 1), PROMPT_POSITIONS // 2, PROMPT_POSITIONS).astype(jnp.int32)
    resp_q = draw_resp_q(jax.random.fold_in(key_of[12], 71), 0)
    resp_k = normal_values(key_of[5], (PROMPT_GROUPS, RESP, KVW), 1.0, 6.0, ((0, 8), (1, 4)))
    resp_v = normal_values(key_of[6], (PROMPT_GROUPS, RESP, KVW), 2.0, 12.0, ((0, 8), (1, 4)))
    resp_len = touch_ends(jax.random.randint(key_of[7], (PROMPT_GROUPS, 2 * N_CTX), 1, RLEN + 1), jax.random.fold_in(key_of[7], 1), 1, RLEN).astype(jnp.int32)
    resp_resid = normal_values(key_of[8], (PROMPT_GROUPS, RESP, D), 0.5, 4.0, ((0, 8), (1, 4)))
    norm_gain = jnp.clip(1.0 + 0.1 * jax.random.normal(key_of[9], (D,), jnp.float32), 0.5, 1.5)
    gate_weight = normal_values(key_of[10], (D, FF), D ** -0.5, 0.09375, ((0, 8), (1, 4)))
    up_weight = normal_values(key_of[11], (D, FF), D ** -0.5, 0.09375, ((0, 8), (1, 4)))
    return dict(prompt_q=prompt_q, prompt_k=prompt_k, prompt_v=prompt_v, prompt_len=prompt_len, resp_q=resp_q, resp_k=resp_k, resp_v=resp_v, resp_len=resp_len, resp_resid=resp_resid, norm_gain=norm_gain, gate_weight=gate_weight, up_weight=up_weight)


def to_heads(token_rows):
    group_count = token_rows.shape[0]
    return token_rows.reshape(group_count, KEY_VALUE_HEADS, QUERY_HEADS // KEY_VALUE_HEADS, HEAD_SIZE).transpose(1, 2, 0, 3).reshape(KEY_VALUE_HEADS, QUERY_HEADS // KEY_VALUE_HEADS * group_count, HEAD_SIZE)

def from_heads(head_rows, group_count):
    return head_rows.reshape(KEY_VALUE_HEADS, QUERY_HEADS // KEY_VALUE_HEADS, group_count, HEAD_SIZE).transpose(2, 0, 1, 3).reshape(group_count, QUERY_HEADS * HEAD_SIZE)

def key_heads(token_rows):
    return token_rows.reshape(token_rows.shape[0], KEY_VALUE_HEADS, HEAD_SIZE).transpose(1, 0, 2)

def attend(queries, key_matrix, values, visible_mask):
    grouped_heads = jnp.tile(visible_mask, (QUERY_HEADS // KEY_VALUE_HEADS, 1))[None]
    scores = jnp.einsum('kqd,ktd->kqt', queries.astype(jnp.float32), key_matrix.astype(jnp.float32)) * HEAD_SIZE ** (-0.5)
    scores = jnp.where(grouped_heads, scores, -1e+30)
    top = lax.optimization_barrier(jnp.max(scores, axis=-1, keepdims=True))
    weights = jnp.where(grouped_heads, jnp.exp(scores - top), 0.0)
    total = lax.optimization_barrier(jnp.sum(weights, axis=-1))
    rounded = lax.optimization_barrier(weights.astype(jnp.bfloat16))
    mixed = jnp.einsum('kqt,ktd->kqd', rounded.astype(jnp.float32), values.astype(jnp.float32))
    return mixed / total[..., None]

def one_group(inputs):
    pq, pk, pv, plen, rq, rk, rv, rlen, resid, gain, gate_weight, up_weight = inputs
    key_matrix = key_heads(pk)
    values = key_heads(pv)
    key_position = jnp.arange(PROMPT_POSITIONS, dtype=jnp.int32)
    attention_block = min(PROMPT_POSITIONS, 512)

    def prompt_block(index):
        start = index * attention_block
        token_rows = lax.dynamic_slice_in_dim(pq, start, attention_block, 0)
        qpos = start + jnp.arange(attention_block, dtype=jnp.int32)
        visible_mask = (key_position[None, :] <= qpos[:, None]) & (key_position[None, :] < plen)
        out = attend(to_heads(token_rows), key_matrix, values, visible_mask)
        return from_heads(out, attention_block).astype(jnp.bfloat16)
    prompt_out = lax.map(prompt_block, jnp.arange(PROMPT_POSITIONS // attention_block, dtype=jnp.int32)).reshape(PROMPT_POSITIONS, QUERY_HEADS * HEAD_SIZE)
    token_rows = jnp.arange(RESP, dtype=jnp.int32)
    slot_r = token_rows // RLEN
    place_r = token_rows % RLEN
    limit = rlen[slot_r]
    prompt_vis = jnp.broadcast_to((key_position < plen)[None, :], (RESP, PROMPT_POSITIONS))
    own_vis = (slot_r[:, None] == slot_r[None, :]) & (place_r[None, :] <= place_r[:, None]) & (place_r[None, :] < limit[None, :])
    visible_mask = jnp.concatenate([prompt_vis, own_vis], axis=1)
    all_keys = jnp.concatenate([key_matrix, key_heads(rk)], axis=1)
    all_values = jnp.concatenate([values, key_heads(rv)], axis=1)
    resp_attn = from_heads(attend(to_heads(rq), all_keys, all_values, visible_mask), RESP).astype(jnp.bfloat16)
    stream = resid.astype(jnp.float32) + resp_attn.astype(jnp.float32)
    scale = lax.rsqrt(lax.optimization_barrier(jnp.mean(stream * stream, axis=-1, keepdims=True)) + 1e-05)
    normed = (stream * scale * gain).astype(jnp.bfloat16)
    gate = jnp.dot(normed, gate_weight, preferred_element_type=jnp.float32)
    up = jnp.dot(normed, up_weight, preferred_element_type=jnp.float32)
    hidden = (jax.nn.silu(gate) * up).astype(jnp.bfloat16)
    return (prompt_out, hidden)

def reference(prompt_q, prompt_k, prompt_v, prompt_len, resp_q, resp_k, resp_v, resp_len, resp_resid, norm_gain, gate_weight, up_weight):
    outs = []
    hiddens = []
    for group in range(PROMPT_GROUPS):
        prompt_out, hidden = one_group((prompt_q[group], prompt_k[group], prompt_v[group], prompt_len[group], resp_q[group], resp_k[group], resp_v[group], resp_len[group], resp_resid[group], norm_gain, gate_weight, up_weight))
        outs.append(prompt_out)
        hiddens.append(hidden)
    return (jnp.stack(outs), jnp.stack(hiddens))
```

```python
import jax
import jax.numpy as jnp
from jax import lax
from jax.sharding import PartitionSpec as P

QUERY_HEADS = 32
KEY_VALUE_HEADS = 4
HEAD_SIZE = 128
RLEN = 16


def to_heads(token_rows):
    group_count = token_rows.shape[0]
    return (
        token_rows.reshape(group_count, KEY_VALUE_HEADS, QUERY_HEADS // KEY_VALUE_HEADS, HEAD_SIZE)
        .transpose(1, 2, 0, 3)
        .reshape(KEY_VALUE_HEADS, QUERY_HEADS // KEY_VALUE_HEADS * group_count, HEAD_SIZE)
    )


def from_heads(head_rows, group_count):
    return (
        head_rows.reshape(KEY_VALUE_HEADS, QUERY_HEADS // KEY_VALUE_HEADS, group_count, HEAD_SIZE)
        .transpose(2, 0, 1, 3)
        .reshape(group_count, QUERY_HEADS * HEAD_SIZE)
    )


def fresh_state(group_count):
    token_rows = QUERY_HEADS // KEY_VALUE_HEADS * group_count
    return (
        jnp.full((KEY_VALUE_HEADS, token_rows), -1e30, jnp.float32),
        jnp.zeros((KEY_VALUE_HEADS, token_rows), jnp.float32),
        jnp.zeros((KEY_VALUE_HEADS, token_rows, HEAD_SIZE), jnp.float32),
    )


def absorb(state, queries, key_rows, value_rows, start, visible_mask_builder):
    length = key_rows.shape[0]
    attention_block = length
    while attention_block > 512 and attention_block % 2 == 0:
        attention_block = attention_block // 2

    def one_block(index, carry):
        top, total, mixed = carry
        offset = index * attention_block
        key_matrix = (
            lax.dynamic_slice_in_dim(key_rows, offset, attention_block, 0)
            .reshape(attention_block, KEY_VALUE_HEADS, HEAD_SIZE)
            .transpose(1, 0, 2)
        )
        values = (
            lax.dynamic_slice_in_dim(value_rows, offset, attention_block, 0)
            .reshape(attention_block, KEY_VALUE_HEADS, HEAD_SIZE)
            .transpose(1, 0, 2)
        )
        key_position = start + offset + jnp.arange(attention_block, dtype=jnp.int32)
        grouped_heads = jnp.tile(
            visible_mask_builder(key_position), (QUERY_HEADS // KEY_VALUE_HEADS, 1)
        )[None]
        scores = jnp.einsum(
            "kqd,ktd->kqt", queries, key_matrix, preferred_element_type=jnp.float32
        ) * HEAD_SIZE ** (-0.5)
        scores = jnp.where(grouped_heads, scores, -1e30)
        newtop = jnp.maximum(top, jnp.max(scores, axis=-1))
        weights = jnp.where(grouped_heads, jnp.exp(scores - newtop[..., None]), 0.0)
        factor = jnp.exp(top - newtop)
        total = total * factor + jnp.sum(weights, axis=-1)
        mixed = mixed * factor[..., None] + jnp.einsum(
            "kqt,ktd->kqd", weights.astype(jnp.bfloat16), values, preferred_element_type=jnp.float32
        )
        return (newtop, total, mixed)

    return lax.fori_loop(0, length // attention_block, one_block, state)


def finish(state, group_count):
    top, total, mixed = state
    return from_heads(mixed / total[..., None], group_count).astype(jnp.bfloat16)


def local(
    prompt_q,
    prompt_k,
    prompt_v,
    prompt_len,
    resp_q,
    resp_k,
    resp_v,
    resp_len,
    resp_resid,
    norm_gain,
    gate_weight,
    up_weight,
):
    dp = lax.axis_size("dp")
    inner = 2 if dp % 2 == 0 else 1
    outer = dp // inner
    dp_here = lax.axis_index("dp")
    z, x = dp_here // inner, dp_here % inner
    depth, width = gate_weight.shape
    parts = 4 if width % 4 == 0 else 1
    part = width // parts
    pair = [(i, i // inner * inner + (i + 1) % inner) for i in range(dp)]
    mine = [
        jnp.concatenate(
            [gate_weight[:, i * part : (i + 1) * part], up_weight[:, i * part : (i + 1) * part]], 1
        )
        for i in range(parts)
    ]
    others = [lax.ppermute(block, "dp", pair) for block in mine] if inner > 1 else None
    ptok = prompt_q.shape[1]
    rtok = resp_q.shape[1]
    here = lax.axis_index("ctx")
    limit = prompt_len[0]
    lens = resp_len[0]
    qpos = here * ptok + jnp.arange(ptok, dtype=jnp.int32)
    prompt_heads = to_heads(prompt_q[0])
    resp_heads = to_heads(resp_q[0])

    def prompt_visible(key_position):
        return (key_position[None, :] <= qpos[:, None]) & (key_position[None, :] < limit)

    def resp_prompt_visible(key_position):
        return jnp.broadcast_to((key_position < limit)[None, :], (rtok, key_position.shape[0]))

    token_rows = jnp.arange(rtok, dtype=jnp.int32)
    slot_r = token_rows // RLEN
    place_r = token_rows % RLEN

    def own_visible(key_position):
        slot_t = key_position // RLEN
        place_t = key_position % RLEN
        bound_t = jnp.where(slot_t == 0, lens[0], lens[1])
        return (
            (slot_r[:, None] == slot_t[None, :])
            & (place_t[None, :] <= place_r[:, None])
            & (place_t[None, :] < bound_t[None, :])
        )

    resp_state = absorb(fresh_state(rtok), resp_heads, resp_k[0], resp_v[0], 0, own_visible)
    pieces = (
        lax.all_gather(prompt_k[0], "ctx", axis=0, tiled=True),
        lax.all_gather(prompt_v[0], "ctx", axis=0, tiled=True),
    )
    prompt_state = absorb(
        fresh_state(ptok), prompt_heads, pieces[0], pieces[1], jnp.int32(0), prompt_visible
    )
    resp_state = absorb(
        resp_state, resp_heads, pieces[0], pieces[1], jnp.int32(0), resp_prompt_visible
    )
    prompt_out = finish(prompt_state, ptok)
    resp_attn = finish(resp_state, rtok)
    stream = resp_resid[0].astype(jnp.float32) + resp_attn.astype(jnp.float32)
    scale = lax.rsqrt(jnp.mean(stream * stream, axis=-1, keepdims=True) + 1e-05)
    normed = (stream * scale * norm_gain).astype(jnp.bfloat16)
    grouped_rows = lax.all_gather(normed, "ctx", axis=0, tiled=True)
    rows = grouped_rows.shape[0]
    columns = jnp.moveaxis(grouped_rows.reshape(rows, outer, inner * depth), 1, 0)
    groups = [[i * inner + j for i in range(outer)] for j in range(inner)]
    if outer > 1:
        columns = lax.all_to_all(columns, "dp", 0, 0, axis_index_groups=groups, tiled=True)
    columns = columns.reshape(outer * rows, inner, depth)
    own_columns = lax.dynamic_index_in_dim(columns, x, 1, keepdims=False)
    other_columns = lax.dynamic_index_in_dim(columns, (x + 1) % inner, 1, keepdims=False)
    hidden_parts = []
    for i in range(parts):
        partial = jnp.dot(own_columns, mine[i], preferred_element_type=jnp.float32)
        if inner > 1:
            partial = partial + jnp.dot(
                other_columns, others[i], preferred_element_type=jnp.float32
            )
        partial = partial.reshape(outer, rows, 2 * part)
        result = lax.dynamic_index_in_dim(partial, z, 0, keepdims=False)
        for way in (1, -1):
            arrived = jnp.zeros((rows, 2 * part), jnp.float32)
            for step in range(outer - 1):
                target = jnp.clip(z + way * (outer - 1 - step), 0, outer - 1)
                term = lax.dynamic_index_in_dim(partial, target, 0, keepdims=False)
                perm = []
                for source in range(outer):
                    rank = source if way == 1 else outer - 1 - source
                    if rank <= step:
                        perm += [
                            (source * inner + j, (source + way) * inner + j) for j in range(inner)
                        ]
                sent = (term + arrived).astype(jnp.bfloat16)
                arrived = lax.ppermute(sent, "dp", perm).astype(jnp.float32)
            result = result + arrived
        gate, up = result[:, :part], result[:, part:]
        hidden_parts.append((jax.nn.silu(gate) * up).astype(jnp.bfloat16))
    hidden = jnp.concatenate(hidden_parts, 1)
    return (prompt_out[None], hidden[None])


def solution(mesh):
    return jax.shard_map(
        local,
        mesh=mesh,
        in_specs=(
            P("dp", "ctx", None),
            P("dp", "ctx", None),
            P("dp", "ctx", None),
            P("dp"),
            P("dp", "ctx", None),
            P("dp", "ctx", None),
            P("dp", "ctx", None),
            P("dp", "ctx"),
            P("dp", "ctx", None),
            P(),
            P("dp", "ctx"),
            P("dp", "ctx"),
        ),
        out_specs=(P("dp", "ctx", None), P("dp", None, "ctx")),
        check_vma=False,
    )
```

```python
import jax
import jax.numpy as jnp
from jax import lax
from jax.sharding import PartitionSpec as P

QUERY_HEADS = 32
KEY_VALUE_HEADS = 4
HEAD_SIZE = 128
RLEN = 16


def to_heads(token_rows):
    group_count = token_rows.shape[0]
    return (
        token_rows.reshape(group_count, KEY_VALUE_HEADS, QUERY_HEADS // KEY_VALUE_HEADS, HEAD_SIZE)
        .transpose(1, 2, 0, 3)
        .reshape(KEY_VALUE_HEADS, QUERY_HEADS // KEY_VALUE_HEADS * group_count, HEAD_SIZE)
    )


def from_heads(head_rows, group_count):
    return (
        head_rows.reshape(KEY_VALUE_HEADS, QUERY_HEADS // KEY_VALUE_HEADS, group_count, HEAD_SIZE)
        .transpose(2, 0, 1, 3)
        .reshape(group_count, QUERY_HEADS * HEAD_SIZE)
    )


def fresh_state(group_count):
    token_rows = QUERY_HEADS // KEY_VALUE_HEADS * group_count
    return (
        jnp.full((KEY_VALUE_HEADS, token_rows), -1e30, jnp.float32),
        jnp.zeros((KEY_VALUE_HEADS, token_rows), jnp.float32),
        jnp.zeros((KEY_VALUE_HEADS, token_rows, HEAD_SIZE), jnp.float32),
    )


def absorb(state, queries, key_rows, value_rows, start, visible_mask_builder):
    length = key_rows.shape[0]
    attention_block = length
    while attention_block > 512 and attention_block % 2 == 0:
        attention_block = attention_block // 2

    def one_block(index, carry):
        top, total, mixed = carry
        offset = index * attention_block
        key_matrix = (
            lax.dynamic_slice_in_dim(key_rows, offset, attention_block, 0)
            .reshape(attention_block, KEY_VALUE_HEADS, HEAD_SIZE)
            .transpose(1, 0, 2)
        )
        values = (
            lax.dynamic_slice_in_dim(value_rows, offset, attention_block, 0)
            .reshape(attention_block, KEY_VALUE_HEADS, HEAD_SIZE)
            .transpose(1, 0, 2)
        )
        key_position = start + offset + jnp.arange(attention_block, dtype=jnp.int32)
        grouped_heads = jnp.tile(
            visible_mask_builder(key_position), (QUERY_HEADS // KEY_VALUE_HEADS, 1)
        )[None]
        scores = jnp.einsum(
            "kqd,ktd->kqt", queries, key_matrix, preferred_element_type=jnp.float32
        ) * HEAD_SIZE ** (-0.5)
        scores = jnp.where(grouped_heads, scores, -1e30)
        newtop = jnp.maximum(top, jnp.max(scores, axis=-1))
        weights = jnp.where(grouped_heads, jnp.exp(scores - newtop[..., None]), 0.0)
        factor = jnp.exp(top - newtop)
        total = total * factor + jnp.sum(weights, axis=-1)
        mixed = mixed * factor[..., None] + jnp.einsum(
            "kqt,ktd->kqd", weights.astype(jnp.bfloat16), values, preferred_element_type=jnp.float32
        )
        return (newtop, total, mixed)

    return lax.fori_loop(0, length // attention_block, one_block, state)


def finish(state, group_count):
    top, total, mixed = state
    return from_heads(mixed / total[..., None], group_count).astype(jnp.bfloat16)


def local(
    prompt_q,
    prompt_k,
    prompt_v,
    prompt_len,
    resp_q,
    resp_k,
    resp_v,
    resp_len,
    resp_resid,
    norm_gain,
    gate_weight,
    up_weight,
):
    dp = lax.axis_size("dp")
    inner = 2 if dp % 2 == 0 else 1
    outer = dp // inner
    dp_here = lax.axis_index("dp")
    z, x = dp_here // inner, dp_here % inner
    depth, width = gate_weight.shape
    parts = 4 if width % 4 == 0 else 1
    part = width // parts
    pair = [(i, i // inner * inner + (i + 1) % inner) for i in range(dp)]
    mine = [
        jnp.concatenate(
            [gate_weight[:, i * part : (i + 1) * part], up_weight[:, i * part : (i + 1) * part]], 1
        )
        for i in range(parts)
    ]
    key_values = jnp.concatenate([prompt_k[0], prompt_v[0]], 1)
    key_values, mine = lax.optimization_barrier((key_values, mine))
    others = [lax.ppermute(block, "dp", pair) for block in mine[:2]]
    ptok = prompt_q.shape[1]
    rtok = resp_q.shape[1]
    here = lax.axis_index("ctx")
    limit = prompt_len[0]
    lens = resp_len[0]
    qpos = here * ptok + jnp.arange(ptok, dtype=jnp.int32)
    prompt_heads = to_heads(prompt_q[0])
    resp_heads = to_heads(resp_q[0])

    def prompt_visible(key_position):
        return (key_position[None, :] <= qpos[:, None]) & (key_position[None, :] < limit)

    def resp_prompt_visible(key_position):
        return jnp.broadcast_to((key_position < limit)[None, :], (rtok, key_position.shape[0]))

    token_rows = jnp.arange(rtok, dtype=jnp.int32)
    slot_r = token_rows // RLEN
    place_r = token_rows % RLEN

    def own_visible(key_position):
        slot_t = key_position // RLEN
        place_t = key_position % RLEN
        bound_t = jnp.where(slot_t == 0, lens[0], lens[1])
        return (
            (slot_r[:, None] == slot_t[None, :])
            & (place_t[None, :] <= place_r[:, None])
            & (place_t[None, :] < bound_t[None, :])
        )

    resp_state = absorb(fresh_state(rtok), resp_heads, resp_k[0], resp_v[0], 0, own_visible)
    pieces = jnp.split(lax.all_gather(key_values, "ctx", axis=0, tiled=True), 2, 1)
    prompt_state = absorb(
        fresh_state(ptok), prompt_heads, pieces[0], pieces[1], jnp.int32(0), prompt_visible
    )
    resp_state = absorb(
        resp_state, resp_heads, pieces[0], pieces[1], jnp.int32(0), resp_prompt_visible
    )
    prompt_out = finish(prompt_state, ptok)
    resp_attn = finish(resp_state, rtok)
    stream = resp_resid[0].astype(jnp.float32) + resp_attn.astype(jnp.float32)
    scale = lax.rsqrt(jnp.mean(stream * stream, axis=-1, keepdims=True) + 1e-05)
    normed = (stream * scale * norm_gain).astype(jnp.bfloat16)
    grouped_rows = lax.all_gather(normed, "ctx", axis=0, tiled=True)
    rows = grouped_rows.shape[0]
    columns = jnp.moveaxis(grouped_rows.reshape(rows, outer, inner * depth), 1, 0)
    groups = [[i * inner + j for i in range(outer)] for j in range(inner)]
    if outer > 1:
        columns = lax.all_to_all(columns, "dp", 0, 0, axis_index_groups=groups, tiled=True)
    columns = columns.reshape(outer * rows, inner, depth)
    own_columns = lax.dynamic_index_in_dim(columns, x, 1, keepdims=False)
    other_columns = lax.dynamic_index_in_dim(columns, (x + 1) % inner, 1, keepdims=False)

    def partial_products(i):
        partial = jnp.dot(own_columns, mine[i], preferred_element_type=jnp.float32)
        if inner > 1:
            partial = partial + jnp.dot(
                other_columns, others[i], preferred_element_type=jnp.float32
            )
        return partial.reshape(outer, rows, 2 * part)

    steps = outer - 1

    def advance(partial, arrived, step):
        result = []
        for way, before in zip((1, -1), arrived):
            target = jnp.clip(z + way * (steps - step), 0, outer - 1)
            sent = lax.dynamic_index_in_dim(partial, target, 0, keepdims=False)
            if before is not None:
                sent = sent + before.astype(jnp.float32)
            perm = []
            for source in range(outer):
                rank = source if way == 1 else outer - 1 - source
                if rank <= step:
                    perm += [
                        (source * inner + j, (source + way) * inner + j) for j in range(inner)
                    ]
            result.append(lax.ppermute(sent.astype(jnp.bfloat16), "dp", perm))
        return tuple(result)

    partials = [None] * parts
    flows = [[(None, None)] for _ in range(parts)]
    hidden_parts = []
    for turn in range(parts + steps):
        if turn < parts:
            if 1 <= turn < parts - 1:
                behind = range(max(turn - 2, 0), turn)
                waited = [flows[i][-1] for i in behind]
                block, waited = lax.optimization_barrier((mine[turn + 1], waited))
                for i, arrived in zip(behind, waited):
                    flows[i][-1] = arrived
                others.append(lax.ppermute(block, "dp", pair))
            partials[turn] = partial_products(turn)
        for i in range(parts):
            step = turn - i
            if 0 <= step < steps:
                flows[i].append(advance(partials[i], flows[i][-1], step))
    for i in range(parts):
        result = lax.dynamic_index_in_dim(partials[i], z, 0, keepdims=False)
        for arrived in flows[i][-1]:
            if arrived is not None:
                result = result + arrived.astype(jnp.float32)
        gate, up = result[:, :part], result[:, part:]
        hidden_parts.append((jax.nn.silu(gate) * up).astype(jnp.bfloat16))
    hidden = jnp.concatenate(hidden_parts, 1)
    return (prompt_out[None], hidden[None])


def solution(mesh):
    return jax.shard_map(
        local,
        mesh=mesh,
        in_specs=(
            P("dp", "ctx", None),
            P("dp", "ctx", None),
            P("dp", "ctx", None),
            P("dp"),
            P("dp", "ctx", None),
            P("dp", "ctx", None),
            P("dp", "ctx", None),
            P("dp", "ctx"),
            P("dp", "ctx", None),
            P(),
            P("dp", "ctx"),
            P("dp", "ctx"),
        ),
        out_specs=(P("dp", "ctx", None), P("dp", None, "ctx")),
        check_vma=False,
    )
```
